32 devices in a mesh: dp: 2 (over x), seq: 4 (over z), mp: 4 (over y, core).
Axes of the slice: x: 2, y: 2, z: 4, core: 2. Of those that a mesh axis runs over, the one named last changes fastest.
Arguments:
- shortening_input: bfloat16 [2, 8192, 2048], P('dp', ('seq', 'mp')), may hold values from -6 to 6
- coarse_grad: bfloat16 [2, 2048, 4096], P('dp', 'seq', 'mp'), may hold values from -6 to 6
- weight_copy: bfloat16 [2, 4096, 4096], P('dp', None, 'mp'), may hold values from -0.0625 to 0.0625
- master: float32 [2, 4096, 4096], P('dp', 'seq', 'mp'), may hold values from -3 to 3
- moment: float32 [2, 4096, 4096], P('dp', 'seq', 'mp'), may hold values from -3 to 3
- second: float32 [2, 4096, 4096], P('dp', 'seq', 'mp'), may hold values from 0.05 to 5
Outputs:
- act_grad: bfloat16 [2, 8192, 2048], P('dp', ('seq', 'mp'))
- new_master: float32 [2, 4096, 4096], P('dp', 'seq', 'mp')
- new_moment: float32 [2, 4096, 4096], P('dp', 'seq', 'mp')
- new_second: float32 [2, 4096, 4096], P('dp', 'seq', 'mp')
- new_weight: bfloat16 [2, 4096, 4096], P(None, 'seq', 'mp')
The draws below stay inside these ranges and needn't reach their ends.
All inputs are finite; a program needn't handle non-finite values.
Results may differ from the reference program's by a relative error of at most 0.009.
Values may be sent and summed in bfloat16 or wider, within the bound.
No kernel may reach another device: no remote copies, remote signals or barrier semaphores. Data moves between devices by JAX's collectives and lax.ppermute only.
A program may use at most 128 MiB of HBM per device.

```python
import math
import jax
import jax.numpy as jnp
from jax import lax

DF = 2048
DC = 4096
SHORT = 4
BATCH = 2
SEQ_LEN = 8192
COARSE = 2048
N_DP = 2
N_SEQ = 4
N_MP = 4


def raised(values, key, source, target, parts, factor):
    def block_of(position):
        return (jnp.arange(values.shape[position]) // (values.shape[position] // parts)).reshape((-1,) + (1,) * (values.ndim - 1 - position))

    one_side = jax.random.permutation(key, parts)[block_of(target)]
    far = (block_of(target) + parts // 2) % parts
    return jnp.where((block_of(source) == one_side) | (block_of(source) == far), factor * values, values)


def levels(own_key, extent, shards, smallest, largest):
    def one(dim, shards_of):
        draws = jax.random.uniform(jax.random.fold_in(jax.random.fold_in(own_key, 6), dim), (shards_of,), jnp.float32, smallest / len(shards), largest / len(shards))
        return jnp.repeat(jnp.exp(draws), extent[dim] // shards_of).reshape((-1,) + (1,) * (len(extent) - dim - 1))

    loudness = one(*shards[0])
    for cut in shards[1:]:
        loudness = loudness * one(*cut)
    return loudness


def centred(own_key, dims, deviation, reach, split=(), held_as=jnp.bfloat16):
    result = jax.random.normal(own_key, dims, jnp.float32) * deviation
    if len(split) > 0:
        result = levels(own_key, dims, split, -0.22, 0.18) * result
    return jnp.clip(result, min=-reach, max=reach).astype(held_as)


def heavy_noise(rng, shape, scale, bound, split, heavy, kind=jnp.bfloat16):
    array = scale * jax.random.normal(rng, shape, jnp.float32)
    if split:
        array = array * levels(rng, shape, split, -0.22, 0.18)
    return jnp.clip(raised(array, jax.random.fold_in(rng, 3), *heavy), -bound, bound).astype(kind)


def setup_inputs(seed: int = 0) -> dict:
    arg_keys = jax.random.split(jax.random.key(seed), 7)
    return {
        "shortening_input": heavy_noise(arg_keys[0], (BATCH, SEQ_LEN, DF), 1.0, 6.0, ((0, 2), (1, 16)), (1, 2, 16, 2.0)),
        "coarse_grad": centred(arg_keys[1], (BATCH, COARSE, DC), 1.0, 6.0, ((0, 2), (1, 4), (2, 4))),
        "weight_copy": centred(arg_keys[2], (N_DP, SHORT * DF // N_DP, DC), (SHORT * DF) ** -0.5, 0.0625, ((0, 2), (2, 4))),
        "master": centred(arg_keys[3], (N_DP, SHORT * DF // N_DP, DC), 0.5, 3.0, ((0, 2), (1, 4), (2, 4)), jnp.float32),
        "moment": centred(arg_keys[4], (N_DP, SHORT * DF // N_DP, DC), 0.5, 3.0, ((0, 2), (1, 4), (2, 4)), jnp.float32),
        "second": jnp.clip(jnp.exp(math.log(5.0) - 4.6051702 * jax.random.uniform(arg_keys[5], (N_DP, SHORT * DF // N_DP, DC), jnp.float32) ** levels(arg_keys[5], (N_DP, SHORT * DF // N_DP, DC), ((0, 2), (1, 4), (2, 4)), -0.2, 0.2)), 0.05, 5.0),
    }


first_beta = 0.9
second_beta = 0.95
first_fix = 1.0 - 0.9 ** 10
second_fix = 1.0 - 0.95 ** 10
adam_eps = 1e-08
learn_rate = 0.05
weight_decay = 0.1

def reference(shortening_input, coarse_grad, weight_copy, master, moment, second):
    sequences = shortening_input.shape[0]
    wide_rows = SHORT * DF
    weights = weight_copy.reshape(wide_rows, DC)
    width = DC // N_MP
    grad_matrix = coarse_grad.reshape(sequences * COARSE, DC)
    accum = jnp.zeros((sequences * COARSE, wide_rows), jnp.float32)
    for block in range(N_MP):
        grad_block = grad_matrix[:, block * width:(block + 1) * width]
        weight_block = weights[:, block * width:(block + 1) * width]
        partial_sum = lax.dot_general(grad_block, weight_block, (((1,), (1,)), ((), ())), preferred_element_type=jnp.float32)
        rounded = lax.optimization_barrier(partial_sum.astype(jnp.bfloat16))
        accum = accum + rounded.astype(jnp.float32)
    fine_grad = accum.reshape(sequences, SEQ_LEN, DF)
    tail_zeros = jnp.zeros((sequences, SHORT - 1, DF), jnp.float32)
    act_grad = jnp.concatenate([fine_grad[:, SHORT - 1:], tail_zeros], axis=1).astype(jnp.bfloat16)
    inputs = shortening_input.reshape(sequences * COARSE, wide_rows)
    block_rows = COARSE // N_SEQ
    block_count = sequences * N_SEQ

    def add_block(index, total):
        start = (index * block_rows).astype(jnp.int32)
        picked = lax.dynamic_slice_in_dim(inputs, start, block_rows, 0)
        grads = lax.dynamic_slice_in_dim(grad_matrix, start, block_rows, 0)
        term = lax.dot_general(picked, grads, (((0,), (0,)), ((), ())), preferred_element_type=jnp.float32)
        rounded = lax.optimization_barrier(term.astype(jnp.bfloat16))
        return total + rounded.astype(jnp.float32)
    summed = lax.fori_loop(0, block_count, add_block, jnp.zeros((wide_rows, DC), jnp.float32))
    weight_grad = (summed * (1.0 / math.sqrt(sequences * COARSE))).reshape(master.shape)
    new_moment = first_beta * moment + (1.0 - first_beta) * weight_grad
    new_second = second_beta * second + (1.0 - second_beta) * weight_grad * weight_grad
    step_ratio = new_moment / first_fix / (jnp.sqrt(new_second / second_fix) + adam_eps)
    new_master = master - learn_rate * (step_ratio + weight_decay * master)
    new_weight = new_master.astype(jnp.bfloat16)
    return (act_grad, new_master, new_moment, new_second, new_weight)
```

```python
import math

import jax
import jax.numpy as jnp
from jax import lax
from jax.sharding import PartitionSpec as P

SHORT = 4
first_beta = 0.9
second_beta = 0.95
first_fix = 1.0 - 0.9**10
second_fix = 1.0 - 0.95**10
adam_eps = 1e-08
learn_rate = 0.05
weight_decay = 0.1
HALVES = 2
PIECES = 4

bf16, f32 = jnp.bfloat16, jnp.float32


def swap(value, axis, step):
    count = lax.axis_size(axis)
    return lax.ppermute(value, axis, [(i, i ^ step) for i in range(count)])


def per_device(shortening_input, coarse_grad, weight_copy, master, moment, second):
    fine = shortening_input[0]
    grad = coarse_grad[0]
    weights = weight_copy[0]
    master, moment, second = master[0], moment[0], second[0]
    rows_dev, features = fine.shape
    coarse_rows, width = grad.shape
    half_rows = weights.shape[0]
    own_rows = rows_dev // SHORT
    block = master.shape[0]
    n_seq, n_mp = lax.axis_size("seq"), lax.axis_size("mp")
    far = n_seq // 2
    x, z, m = lax.axis_index("dp"), lax.axis_index("seq"), lax.axis_index("mp")
    h, l = z // 2, z % 2

    t = lax.broadcasted_iota(jnp.int32, (rows_dev, rows_dev), 0)
    u = lax.broadcasted_iota(jnp.int32, (rows_dev, rows_dev), 1)
    spread = (u == SHORT * (t % own_rows) + t // own_rows).astype(bf16)
    planes = jnp.dot(spread, fine, preferred_element_type=f32).astype(bf16)

    def part(dp, hi, lo):
        offset = dp * half_rows + (2 * hi + lo) * block
        return lax.dynamic_slice(
            planes, (offset // features * own_rows, offset % features), (own_rows, block)
        )

    def gather_inputs(hi):
        blocks = [
            part(x, hi, l),
            swap(part(1 - x, hi, l), "dp", 1),
            swap(part(x, hi, 1 - l), "seq", 1),
            lax.ppermute(
                part(1 - x, hi, 1 - l),
                ("dp", "seq"),
                [(i, i ^ n_seq ^ 1) for i in range(2 * n_seq)],
            ),
        ]
        own = jnp.concatenate(blocks, axis=0)
        across = swap(own, "mp", 2)
        beside = swap(own, "mp", 1)
        both = swap(across, "mp", 1)
        return jnp.concatenate([both, beside, across, own], axis=0)

    order = (3, 1, 2, 0)
    grads = jnp.concatenate(
        [lax.dynamic_slice_in_dim(grad, (m ^ j) * own_rows, own_rows, 0) for j in order], axis=0
    )
    piece = width // HALVES

    def gather_grads(k):
        mine = grads[:, k * piece : (k + 1) * piece]
        other = swap(mine, "dp", 1)
        return [mine, other, swap(mine, "seq", 1), swap(other, "seq", 1)]

    def tokens(parts):
        return jnp.stack([v.reshape(n_mp, own_rows, piece) for v in parts], axis=1).reshape(
            -1, piece
        )

    def against(a, b):
        return lax.dot_general(a, b, (((0,), (0,)), ((), ())), preferred_element_type=f32)

    def act_partial(rows):
        return lax.dot_general(
            rows, weights, (((1,), (1,)), ((), ())), preferred_element_type=f32
        ).astype(bf16)

    def act_sum(rows):
        partial = act_partial(rows)
        cut = 2 * own_rows
        pair = partial[cut:].astype(f32) + swap(partial[:cut], "mp", 1).astype(f32)
        send = pair[:own_rows].astype(bf16)
        return pair[own_rows:] + swap(send, "mp", 2).astype(f32)

    x_far = {}
    for k in range(1, far):
        x_far[k] = gather_inputs((h + k) % far)
    g = [gather_grads(0)]
    x_far[0] = gather_inputs(h)
    g += [gather_grads(k) for k in range(1, HALVES)]
    act_own = act_sum(grads).astype(bf16)
    other_grads = jnp.concatenate([v[1] for v in g], axis=1)
    act_other = swap(act_sum(other_grads).astype(bf16), "dp", 1)

    mine = act_own.reshape(own_rows, 2, features)
    theirs = act_other.reshape(own_rows, 2, features)
    stack = jnp.concatenate([mine[:, 0], mine[:, 1], theirs[:, 0], theirs[:, 1]], axis=0)
    first = jnp.stack([mine[0], theirs[0]])
    first = lax.dynamic_index_in_dim(first, x, 0, False), lax.dynamic_index_in_dim(first, 1 - x, 0, False)
    first = jnp.concatenate(first, axis=0)[: SHORT - 1]
    count = n_seq * n_mp
    later = lax.ppermute(first, ("seq", "mp"), [(i, i - 1) for i in range(1, count)])
    stack = jnp.concatenate([stack, jnp.pad(later, ((0, 8 - (SHORT - 1)), (0, 0)))], axis=0)
    t = lax.broadcasted_iota(jnp.int32, (rows_dev, rows_dev + 8), 0) + SHORT - 1
    u = lax.broadcasted_iota(jnp.int32, (rows_dev, rows_dev + 8), 1)
    p, r = t % SHORT, t // SHORT
    source = ((p + 2 * x) % SHORT) * own_rows + r
    source = jnp.where(t < rows_dev, source, t)
    gather = (u == source).astype(bf16)
    act_grad = jnp.dot(gather, stack, preferred_element_type=f32).astype(bf16)

    scale = 1.0 / math.sqrt(lax.axis_size("dp") * coarse_rows * n_seq)
    g_all = [tokens(v) for v in g]
    cols = width // PIECES
    per = PIECES // HALVES
    outs = []
    for i in range(PIECES):
        rhs = g_all[i // per][:, (i % per) * cols : (i % per + 1) * cols]
        total = None
        for k in range(1, far):
            sent = against(x_far[k], rhs).astype(bf16)
            came = lax.ppermute(
                sent, "seq", [(s, (s + 2 * k) % n_seq) for s in range(n_seq)]
            ).astype(f32)
            total = came if total is None else total + came
        own = against(x_far[0], rhs)
        gradient = (own if total is None else own + total) * scale
        at = slice(i * cols, (i + 1) * cols)
        new_moment = first_beta * moment[:, at] + (1.0 - first_beta) * gradient
        new_second = second_beta * second[:, at] + (1.0 - second_beta) * gradient * gradient
        ratio = new_moment / first_fix / (jnp.sqrt(new_second / second_fix) + adam_eps)
        new_master = master[:, at] - learn_rate * (ratio + weight_decay * master[:, at])
        low = new_master.astype(bf16)
        other = swap(low, "dp", 1)
        outs.append((new_master, new_moment, new_second, low, other))
    new_master, new_moment, new_second, low, other = [
        jnp.concatenate(v, axis=1) for v in zip(*outs)
    ]
    new_weight = jnp.stack([jnp.where(x == 0, low, other), jnp.where(x == 0, other, low)])
    return (act_grad[None], new_master[None], new_moment[None], new_second[None], new_weight)


def solution(mesh):
    return jax.shard_map(
        per_device,
        mesh=mesh,
        in_specs=(
            P("dp", ("seq", "mp"), None),
            P("dp", "seq", "mp"),
            P("dp", None, "mp"),
            P("dp", "seq", "mp"),
            P("dp", "seq", "mp"),
            P("dp", "seq", "mp"),
        ),
        out_specs=(
            P("dp", ("seq", "mp"), None),
            P("dp", "seq", "mp"),
            P("dp", "seq", "mp"),
            P("dp", "seq", "mp"),
            P(None, "seq", "mp"),
        ),
        check_vma=False,
    )
```

```python
import functools
import math

import jax
import jax.numpy as jnp
from jax import lax
from jax.experimental import pallas as pl
from jax.experimental.pallas import tpu as pltpu
from jax.sharding import PartitionSpec as P

SHORT = 4
first_beta = 0.9
second_beta = 0.95
first_fix = 1.0 - 0.9**10
second_fix = 1.0 - 0.95**10
adam_eps = 1e-08
learn_rate = 0.05
weight_decay = 0.1
PIECES = 4

bf16, f32 = jnp.bfloat16, jnp.float32


def swap(value, axis, step):
    count = lax.axis_size(axis)
    return lax.ppermute(value, axis, [(i, i ^ step) for i in range(count)])


def launch(kernel, values, out, grid=(), in_specs=None, out_specs=None, scalars=(), aliases=None, after=(), limit=14):
    whole = pl.BlockSpec(memory_space=pltpu.VMEM)
    taken = len(scalars) + len(values)

    def body(*refs):
        kernel(*refs[:taken], *refs[taken + len(after) :])

    return pl.pallas_call(
        body,
        grid_spec=pltpu.PrefetchScalarGridSpec(
            num_scalar_prefetch=len(scalars),
            grid=grid,
            in_specs=(in_specs or [whole] * len(values))
            + [pl.BlockSpec(memory_space=pl.ANY)] * len(after),
            out_specs=out_specs or [whole] * len(out),
        ),
        out_shape=[jax.ShapeDtypeStruct(shape, dtype) for shape, dtype in out],
        input_output_aliases=aliases or {},
        compiler_params=pltpu.CompilerParams(vmem_limit_bytes=limit * 2**20),
        cost_estimate=pl.CostEstimate(flops=1, bytes_accessed=1, transcendentals=0),
    )(*scalars, *values, *after)


def sort_kernel(order, m_ref, grad_ref, sent_ref, kept_ref, *piece_refs):
    count = grad_ref.shape[0] // len(order)
    half = len(order) // 2
    for i, j in enumerate(order):
        start = pl.multiple_of((m_ref[0] ^ j) * count, count)
        rows = grad_ref[pl.ds(start, count), :]
        ref, at = (sent_ref, i) if i < half else (kept_ref, i - half)
        ref[at * count : (at + 1) * count, :] = rows
        first = 0
        for ref in piece_refs:
            ref[i * count : (i + 1) * count, :] = rows[:, first : first + ref.shape[1]]
            first += ref.shape[1]


def halves_kernel(own_ref, first_ref, later_ref, sent_ref, kept_ref, *pack_refs):
    count, split = sent_ref.shape[0], first_ref.shape[1]
    for ref, part in ((sent_ref, slice(0, count)), (kept_ref, slice(count, 2 * count))):
        ref[:, :split] = first_ref[part]
        ref[:, split:] = later_ref[part]
    for i, ref in enumerate(pack_refs):
        at = slice(i * ref.shape[1], (i + 1) * ref.shape[1])
        ref[: 2 * count] = own_ref[:, at]
        ref[2 * count :] = later_ref[:, at]


def split_kernel(rows, block, at_ref, fine_ref, *out_refs):
    count = fine_ref.shape[0]
    r = lax.broadcasted_iota(jnp.int32, (rows, count), 0)
    t = lax.broadcasted_iota(jnp.int32, (rows, count), 1)
    i = 0
    for out_ref in out_refs:
        for k in range(out_ref.shape[0] // rows):
            pick = jnp.where(t == SHORT * r + at_ref[2 * i], 1.0, 0.0).astype(bf16)
            columns = pl.ds(pl.multiple_of(at_ref[2 * i + 1] * block, block), block)
            out_ref[k * rows : (k + 1) * rows, :] = jnp.dot(
                pick, fine_ref[:, columns], preferred_element_type=f32
            ).astype(bf16)
            i += 1


def stack_kernel(picks, *refs):
    count = len(refs) - len(picks)
    for pick, out_ref in zip(picks, refs[count:]):
        at = 0
        for i, first, size in pick:
            out_ref[at : at + size, :] = refs[i][first : first + size, :]
            at += size


def stack(picks, *values, after=()):
    out = [
        ((sum(size for _, _, size in pick), values[pick[0][0]].shape[1]), bf16) for pick in picks
    ]
    return launch(functools.partial(stack_kernel, picks), values, out, after=after)


def act_kernel(a_ref, b_ref, w_ref, pair_ref, send_ref, rest_ref):
    count = send_ref.shape[0]
    product = 0.0
    for rows, part in ((a_ref, w_ref), (b_ref, pair_ref)):
        product += lax.dot_general(
            rows[...], part[...], (((1,), (1,)), ((), ())), preferred_element_type=f32
        )
    send_ref[...] = product[:count].astype(bf16)
    rest_ref[...] = product[count:]


def act_products(rows, weights, after=()):
    count = rows[0].shape[0] // 2
    wide, depth = weights[0].shape
    step = 512
    return launch(
        act_kernel,
        [*rows, *weights],
        [((count, wide), bf16), ((count, wide), f32)],
        grid=(wide // step,),
        in_specs=[pl.BlockSpec(v.shape, lambda i: (0, 0)) for v in rows]
        + [pl.BlockSpec((step, depth), lambda i: (i, 0))] * 2,
        out_specs=[pl.BlockSpec((count, step), lambda i: (0, i))] * 2,
        after=after,
    )


def last_kernel(keep_ref, came_ref, out_ref):
    out_ref[...] = (keep_ref[...] + came_ref[...].astype(f32)).astype(bf16)


def last_sum(keep, came, after=()):
    return launch(last_kernel, [keep, came], [(keep.shape, bf16)], after=after)[0]


def against_kernel(groups, places, *refs):
    x_refs, g_refs, out_ref = refs[: sum(groups)], refs[sum(groups) : -1], refs[-1]
    count = x_refs[0].shape[0] * groups[0] // len(places)
    total, first = None, 0
    for j, size in enumerate(groups):
        x = jnp.concatenate([ref[...] for ref in x_refs[first : first + size]], axis=0)
        first += size
        g = jnp.concatenate(
            [
                g_refs[i][row + j * count : row + (j + 1) * count, at : at + out_ref.shape[1]]
                for i, row, at in places
            ],
            axis=0,
        )
        part = lax.dot_general(x, g, (((0,), (0,)), ((), ())), preferred_element_type=f32)
        total = part if total is None else total + part
    out_ref[...] = total.astype(out_ref.dtype)


def against(x, g, cols, dtype, after=()):
    values, places = g
    groups = [len(v) for v in x]
    flat = [v for group in x for v in group]
    return launch(
        functools.partial(against_kernel, groups, places),
        [*flat, *values],
        [((flat[0].shape[1], cols), dtype)],
        after=after,
        limit=20,
    )[0]


def adam_kernel(scale, first, *refs):
    x_ref, own, came, master, moment, second = refs[:6]
    new_master, new_moment, new_second, new_weight, low = refs[6 if first else 10 :]
    gradient = (own[...] + came[...].astype(f32)) * scale
    m = first_beta * moment[...] + (1.0 - first_beta) * gradient
    s = second_beta * second[...] + (1.0 - second_beta) * gradient * gradient
    ratio = m / first_fix / (jnp.sqrt(s / second_fix) + adam_eps)
    w = master[...] - learn_rate * (ratio + weight_decay * master[...])
    new_master[...] = w
    new_moment[...] = m
    new_second[...] = s
    low[...] = w.astype(bf16)
    new_weight[0] = w.astype(bf16)


def adam(x, own, came, state, i, scale, held, after=()):
    rows, cols = own.shape
    wide = state[0].shape[1]
    step = min(256, rows)
    local = pl.BlockSpec((step, cols), lambda r, x: (r, 0))
    whole = pl.BlockSpec((step, cols), lambda r, x: (r, i))
    weight = pl.BlockSpec((1, step, cols), lambda r, x: (x[0], r, i))
    first = held is None
    return launch(
        functools.partial(adam_kernel, scale, first),
        [own, came, *state, *(held or ())],
        [((rows, wide), f32)] * 3 + [((2, rows, wide), bf16), ((rows, cols), bf16)],
        grid=(rows // step,),
        in_specs=[local, local, whole, whole, whole]
        + ([] if first else [pl.BlockSpec(memory_space=pl.ANY)] * 4),
        out_specs=[whole, whole, whole, weight, local],
        scalars=(x.reshape(1),),
        aliases={} if first else {6: 0, 7: 1, 8: 2, 9: 3},
        after=after,
    )


def place_kernel(x_ref, other_ref, held_ref, out_ref):
    out_ref[0] = other_ref[...]


def place_other(x, other, held, column, after=()):
    rows, cols = other.shape
    return launch(
        place_kernel,
        [other, held],
        [(held.shape, held.dtype)],
        grid=(1,),
        in_specs=[
            pl.BlockSpec((rows, cols), lambda r, x: (0, 0)),
            pl.BlockSpec(memory_space=pl.ANY),
        ],
        out_specs=[pl.BlockSpec((1, rows, cols), lambda r, x: (1 - x[0], 0, column))],
        scalars=(x.reshape(1),),
        aliases={2: 0},
        after=after,
    )[0]


def merge_kernel(x_ref, own_ref, other_ref, later_ref, out_ref):
    rows, features = out_ref.shape
    count = own_ref.shape[0]
    t = lax.broadcasted_iota(jnp.int32, (rows, count), 0) + SHORT - 1
    u = lax.broadcasted_iota(jnp.int32, (rows, count), 1)
    e = lax.broadcasted_iota(jnp.int32, (rows, later_ref.shape[0]), 0) + SHORT - 1
    v = lax.broadcasted_iota(jnp.int32, (rows, later_ref.shape[0]), 1)
    x = x_ref[0]
    picks = [
        jnp.where(t == SHORT * u + 2 * side + q, 1.0, 0.0).astype(bf16)
        for side in (x, 1 - x)
        for q in range(2)
    ]
    tail = jnp.where(e == rows + v, 1.0, 0.0).astype(bf16)
    step = 512
    for at in range(0, features, step):
        total = jnp.dot(tail, later_ref[:, at : at + step], preferred_element_type=f32)
        for i, ref in enumerate((own_ref, own_ref, other_ref, other_ref)):
            plane = ref[:, i % 2 * features + at : i % 2 * features + at + step]
            total += jnp.dot(picks[i], plane, preferred_element_type=f32)
        out_ref[:, at : at + step] = total.astype(bf16)


def merge(x, own, other, later, after=()):
    rows = own.shape[0] * SHORT
    return launch(
        merge_kernel,
        [own, other, later],
        [((rows, own.shape[1] // 2), bf16)],
        scalars=(x.reshape(1),),
        after=after,
        limit=20,
    )[0]


def per_device(shortening_input, coarse_grad, weight_copy, master, moment, second):
    fine = shortening_input[0]
    grad = coarse_grad[0]
    weights = weight_copy[0]
    state = (master[0], moment[0], second[0])
    rows_dev, features = fine.shape
    coarse_rows, width = grad.shape
    half_rows = weights.shape[0]
    one = rows_dev // SHORT
    block = master.shape[1]
    n_seq, n_mp = lax.axis_size("seq"), lax.axis_size("mp")
    far = n_seq // 2
    x, z, m = lax.axis_index("dp"), lax.axis_index("seq"), lax.axis_index("mp")
    h, l = z // 2, z % 2
    cols = width // PIECES
    order = (3, 1, 2, 0)

    def place(dp, hi, lo):
        offset = dp * half_rows + (2 * hi + lo) * block
        return [offset // features, offset % features // block]

    def cut(hi, sizes, after):
        places = [place(x, hi, l), place(x, hi, 1 - l), place(1 - x, hi, l), place(1 - x, hi, 1 - l)]
        places = jnp.stack([v for p in places for v in p]).astype(jnp.int32)
        return launch(
            functools.partial(split_kernel, one, block),
            [fine],
            [((size * one, block), bf16) for size in sizes],
            scalars=(places,),
            after=after,
        )

    def diagonal(v):
        return lax.ppermute(v, ("dp", "seq"), [(i, i ^ n_seq ^ 1) for i in range(2 * n_seq)])

    def ahead(v, k):
        return lax.ppermute(v, "seq", [(s, (s + 2 * k) % n_seq) for s in range(n_seq)])

    pair_weights = swap(weights, "mp", 1)
    pair_send, own_rows, g0, g_later = launch(
        functools.partial(sort_kernel, order),
        [grad],
        [((2 * one, width), bf16)] * 2
        + [((coarse_rows, cols), bf16), ((coarse_rows, width - cols), bf16)],
        scalars=(m.reshape(1),),
    )
    g0_dp = swap(g0, "dp", 1)
    first = {}
    last = g0
    for k in range(1, far):
        own, to_seq, to_dp, to_both = cut((h + k) % far, (1, 1, 1, 1), [last])
        first[k] = own, swap(to_dp, "dp", 1), swap(to_seq, "seq", 1), diagonal(to_both)
        last = own
    for k, v in first.items():
        mine, pack = stack(
            [[(i, 0, one) for i in range(4)], [(4, 0, coarse_rows), (5, 0, coarse_rows)]],
            *v, g0, g0_dp, after=[last, pair_weights],
        )
        first[k] = mine, swap(mine, "mp", 1), swap(mine, "mp", 2)
        last = mine
    packs = [swap(pack, "seq", 1)]
    later_dp = swap(g_later, "dp", 1)
    own_pair = swap(pair_send, "mp", 1)
    own_send, own_rest = act_products([own_rows, own_pair], [weights, pair_weights], [last])
    own_came = swap(own_send, "mp", 2)
    last = own_rest
    other_send, other_rows, *later_packs = launch(
        halves_kernel,
        [g_later, g0_dp, later_dp],
        [((2 * one, width), bf16)] * 2 + [((2 * coarse_rows, cols), bf16)] * (PIECES - 1),
        after=[last, packs[0]] + [v[1] for v in first.values()],
    )
    packs += [swap(v, "seq", 1) for v in later_packs]
    other_pair = swap(other_send, "mp", 1)
    own, to_seq, to_dp = cut(h, (1, 1, 2), [other_rows])
    x_dp = swap(to_dp, "dp", 1)
    last = own
    x_far = {}
    for k, (mine, beside, across) in first.items():
        (across,) = stack([[(0, 0, 4 * one)]], across, after=[last])
        x_far[k] = [swap(across, "mp", 1)], [beside], [across], [mine]
        last = across
    other_send, other_rest = act_products([other_rows, other_pair], [weights, pair_weights], [last])
    other_came = swap(other_send, "mp", 2)
    last = other_rest

    def gradients(i):
        if i == 0:
            return [g0, g0_dp, packs[0]], [(0, 0, 0), (1, 0, 0), (2, 0, 0), (2, coarse_rows, 0)]
        at = (i - 1) * cols
        return [g_later, later_dp, packs[i]], [(0, 0, at), (1, 0, at), (2, 0, 0), (2, coarse_rows, 0)]

    def far_sums(i, after):
        came = []
        for k, v in x_far.items():
            sent = against(v, gradients(i), cols, bf16, after=after)
            came.append(ahead(sent, k))
            after = [sent]
        return (came[0] if far == 2 else sum(v.astype(f32) for v in came)), sent

    sums = {}
    sums[0], last = far_sums(0, [last, packs[1]])
    near, to_seq = stack(
        [[(0, 0, one), (2, 0, one)], [(1, 0, one), (2, one, one)]], own, to_seq, x_dp, after=[last]
    )
    x_seq = swap(to_seq, "seq", 1)
    (mine,) = stack([[(0, 0, 2 * one), (1, 0, 2 * one)]], near, x_seq, after=[sums[0]])
    across, beside = swap(mine, "mp", 2), swap(mine, "mp", 1)
    sums[1], last = far_sums(1, [mine])
    act_other = last_sum(other_rest, other_came, after=[last])
    act_other_came = swap(act_other, "dp", 1)
    (across,) = stack([[(0, 0, 4 * one)]], across, after=[act_other, act_other_came, beside, sums[1], packs[2]])
    both = swap(across, "mp", 1)
    x_near = [both], [beside], [across], [mine]
    sums[2], last = far_sums(2, [across])
    scale = 1.0 / math.sqrt(lax.axis_size("dp") * coarse_rows * n_seq)
    held, others = None, []

    def nearby(i, after):
        return against(x_near, gradients(i), cols, f32, after=after)

    def update(i, gradient, after):
        nonlocal held
        *held, low = adam(x, gradient, sums[i], state, i, scale, held, after=after)
        others.append(swap(low, "dp", 1))
        return low

    last = update(0, nearby(0, [last]), [])
    last = update(1, nearby(1, [last]), [])
    sums[3], last = far_sums(3, [last, sums[2]])
    last = update(2, nearby(2, [last]), [])
    gradient = nearby(3, [last])

    def put(i, after):
        held[3] = place_other(x, others[i], held[3], i, after=after)

    put(0, [gradient])
    put(1, [])
    act_own = last_sum(own_rest, own_came, after=[held[3]])
    head = jnp.where(
        x == 0,
        jnp.concatenate([act_own[:1], act_other_came[:1]], axis=1),
        jnp.concatenate([act_other_came[:1], act_own[:1]], axis=1),
    )
    head = head[:, : (SHORT - 1) * features].reshape(SHORT - 1, features)
    count = n_seq * n_mp
    later = lax.ppermute(head, ("seq", "mp"), [(s, s - 1) for s in range(1, count)])
    later = jnp.pad(later, ((0, 16 - (SHORT - 1)), (0, 0)))
    act_grad = merge(x, act_own, act_other_came, later)
    last = update(3, gradient, [act_grad])
    put(2, [last])
    put(3, [])
    new_master, new_moment, new_second, new_weight = held
    return (act_grad[None], new_master[None], new_moment[None], new_second[None], new_weight)


def solution(mesh):
    return jax.shard_map(
        per_device,
        mesh=mesh,
        in_specs=(
            P("dp", ("seq", "mp"), None),
            P("dp", "seq", "mp"),
            P("dp", None, "mp"),
            P("dp", "seq", "mp"),
            P("dp", "seq", "mp"),
            P("dp", "seq", "mp"),
        ),
        out_specs=(
            P("dp", ("seq", "mp"), None),
            P("dp", "seq", "mp"),
            P("dp", "seq", "mp"),
            P("dp", "seq", "mp"),
            P(None, "seq", "mp"),
        ),
        check_vma=False,
    )
```

```python
import functools
import math

import jax
import jax.numpy as jnp
from jax import lax
from jax.experimental import pallas as pl
from jax.experimental.pallas import tpu as pltpu
from jax.sharding import PartitionSpec as P

SHORT = 4
first_beta = 0.9
second_beta = 0.95
first_fix = 1.0 - 0.9**10
second_fix = 1.0 - 0.95**10
adam_eps = 1e-08
learn_rate = 0.05
weight_decay = 0.1
PIECES = 4

bf16, f32 = jnp.bfloat16, jnp.float32


def swap(value, axis, step):
    count = lax.axis_size(axis)
    return lax.ppermute(value, axis, [(i, i ^ step) for i in range(count)])


def launch(kernel, values, out, grid=(), in_specs=None, out_specs=None, scalars=(), aliases=None, after=(), limit=14, span=0):
    whole = pl.BlockSpec(memory_space=pltpu.VMEM)
    taken = len(scalars) + len(values)

    def body(*refs):
        kernel(*refs[:taken], *refs[taken + len(after) :])

    return pl.pallas_call(
        body,
        grid_spec=pltpu.PrefetchScalarGridSpec(
            num_scalar_prefetch=len(scalars),
            grid=grid,
            in_specs=(in_specs or [whole] * len(values))
            + [pl.BlockSpec(memory_space=pl.ANY)] * len(after),
            out_specs=out_specs or [whole] * len(out),
        ),
        out_shape=[jax.ShapeDtypeStruct(shape, dtype) for shape, dtype in out],
        input_output_aliases=aliases or {},
        compiler_params=pltpu.CompilerParams(vmem_limit_bytes=limit * 2**20),
        cost_estimate=pl.CostEstimate(flops=1 + span * 1200000000, bytes_accessed=1 + span * 3500000, transcendentals=0),
    )(*scalars, *values, *after)


def mark_kernel(out_ref):
    out_ref[...] = jnp.zeros_like(out_ref)


def mark(span, *after):
    return launch(mark_kernel, [], [((8, 128), f32)], after=after, span=span)[0]


def sort_kernel(order, m_ref, grad_ref, sent_ref, kept_ref, *piece_refs):
    count = grad_ref.shape[0] // len(order)
    half = len(order) // 2
    for i, j in enumerate(order):
        start = pl.multiple_of((m_ref[0] ^ j) * count, count)
        rows = grad_ref[pl.ds(start, count), :]
        ref, at = (sent_ref, i) if i < half else (kept_ref, i - half)
        ref[at * count : (at + 1) * count, :] = rows
        first = 0
        for ref in piece_refs:
            ref[i * count : (i + 1) * count, :] = rows[:, first : first + ref.shape[1]]
            first += ref.shape[1]


def halves_kernel(own_ref, first_ref, later_ref, sent_ref, kept_ref, *pack_refs):
    count, split = sent_ref.shape[0], first_ref.shape[1]
    for ref, part in ((sent_ref, slice(0, count)), (kept_ref, slice(count, 2 * count))):
        ref[:, :split] = first_ref[part]
        ref[:, split:] = later_ref[part]
    for i, ref in enumerate(pack_refs):
        at = slice(i * ref.shape[1], (i + 1) * ref.shape[1])
        ref[: 2 * count] = own_ref[:, at]
        ref[2 * count :] = later_ref[:, at]


def split_kernel(rows, block, at_ref, fine_ref, *out_refs):
    count = fine_ref.shape[0]
    r = lax.broadcasted_iota(jnp.int32, (rows, count), 0)
    t = lax.broadcasted_iota(jnp.int32, (rows, count), 1)
    i = 0
    for out_ref in out_refs:
        for k in range(out_ref.shape[0] // rows):
            pick = jnp.where(t == SHORT * r + at_ref[2 * i], 1.0, 0.0).astype(bf16)
            columns = pl.ds(pl.multiple_of(at_ref[2 * i + 1] * block, block), block)
            out_ref[k * rows : (k + 1) * rows, :] = jnp.dot(
                pick, fine_ref[:, columns], preferred_element_type=f32
            ).astype(bf16)
            i += 1


def stack_kernel(picks, *refs):
    count = len(refs) - len(picks)
    for pick, out_ref in zip(picks, refs[count:]):
        at = 0
        for i, first, size in pick:
            out_ref[at : at + size, :] = refs[i][first : first + size, :]
            at += size


def stack(picks, *values, after=()):
    out = [
        ((sum(size for _, _, size in pick), values[pick[0][0]].shape[1]), bf16) for pick in picks
    ]
    return launch(functools.partial(stack_kernel, picks), values, out, after=after)


def act_kernel(a_ref, b_ref, w_ref, pair_ref, *out_refs):
    *send_refs, rest_ref = out_refs
    count = rest_ref.shape[0]
    product = 0.0
    for rows, part in ((a_ref, w_ref), (b_ref, pair_ref)):
        product += lax.dot_general(
            rows[...], part[...], (((1,), (1,)), ((), ())), preferred_element_type=f32
        )
    rest_ref[...] = product[count:]
    half = pl.num_programs(0) // 2
    for i, ref in enumerate(send_refs):

        @pl.when(pl.program_id(0) // half == i)
        def _():
            ref[...] = product[:count].astype(bf16)


def act_products(rows, weights, after=()):
    count = rows[0].shape[0] // 2
    wide, depth = weights[0].shape
    step = 512
    half = wide // step // 2
    return launch(
        act_kernel,
        [*rows, *weights],
        [((count, wide // 2), bf16)] * 2 + [((count, wide), f32)],
        grid=(wide // step,),
        in_specs=[pl.BlockSpec(v.shape, lambda i: (0, 0)) for v in rows]
        + [pl.BlockSpec((step, depth), lambda i: (i, 0))] * 2,
        out_specs=[
            pl.BlockSpec((count, step), lambda i: (0, jnp.minimum(i, half - 1))),
            pl.BlockSpec((count, step), lambda i: (0, jnp.maximum(i - half, 0))),
            pl.BlockSpec((count, step), lambda i: (0, i)),
        ],
        after=after,
    )


def last_kernel(keep_ref, *refs):
    *came_refs, out_ref = refs
    at = 0
    for ref in came_refs:
        part = slice(at, at + ref.shape[1])
        out_ref[:, part] = (keep_ref[:, part] + ref[...].astype(f32)).astype(bf16)
        at += ref.shape[1]


def last_sum(keep, came, after=()):
    return launch(last_kernel, [keep, *came], [(keep.shape, bf16)], after=after)[0]


def against_kernel(groups, places, *refs):
    x_refs, g_refs, out_ref = refs[: sum(groups)], refs[sum(groups) : -1], refs[-1]
    count = sum(ref.shape[0] for ref in x_refs[: groups[0]]) // len(places)
    total, first = None, 0
    for j, size in enumerate(groups):
        x = jnp.concatenate([ref[...] for ref in x_refs[first : first + size]], axis=0)
        first += size
        g = jnp.concatenate(
            [
                g_refs[i][row + j * count : row + (j + 1) * count, at : at + out_ref.shape[1]]
                for i, row, at in places
            ],
            axis=0,
        )
        part = lax.dot_general(x, g, (((0,), (0,)), ((), ())), preferred_element_type=f32)
        total = part if total is None else total + part
    out_ref[...] = total.astype(out_ref.dtype)


def against(x, g, cols, dtype, after=()):
    values, places = g
    groups = [len(v) for v in x]
    flat = [v for group in x for v in group]
    return launch(
        functools.partial(against_kernel, groups, places),
        [*flat, *values],
        [((flat[0].shape[1], cols), dtype)],
        after=after,
        limit=20,
    )[0]


def adam_kernel(scale, first, *refs):
    x_ref, own, came, master, moment, second = refs[:6]
    new_master, new_moment, new_second, new_weight, low = refs[6 if first else 10 :]
    gradient = (own[...] + came[...].astype(f32)) * scale
    m = first_beta * moment[...] + (1.0 - first_beta) * gradient
    s = second_beta * second[...] + (1.0 - second_beta) * gradient * gradient
    ratio = m / first_fix / (jnp.sqrt(s / second_fix) + adam_eps)
    w = master[...] - learn_rate * (ratio + weight_decay * master[...])
    new_master[...] = w
    new_moment[...] = m
    new_second[...] = s
    low[...] = w.astype(bf16)
    new_weight[0] = w.astype(bf16)


def adam(x, own, came, state, i, scale, held, after=()):
    rows, cols = own.shape
    wide = state[0].shape[1]
    step = min(256, rows)
    local = pl.BlockSpec((step, cols), lambda r, x: (r, 0))
    whole = pl.BlockSpec((step, cols), lambda r, x: (r, i))
    weight = pl.BlockSpec((1, step, cols), lambda r, x: (x[0], r, i))
    first = held is None
    return launch(
        functools.partial(adam_kernel, scale, first),
        [own, came, *state, *(held or ())],
        [((rows, wide), f32)] * 3 + [((2, rows, wide), bf16), ((rows, cols), bf16)],
        grid=(rows // step,),
        in_specs=[local, local, whole, whole, whole]
        + ([] if first else [pl.BlockSpec(memory_space=pl.ANY)] * 4),
        out_specs=[whole, whole, whole, weight, local],
        scalars=(x.reshape(1),),
        aliases={} if first else {6: 0, 7: 1, 8: 2, 9: 3},
        after=after,
    )


def place_kernel(x_ref, *refs):
    *other_refs, held_ref, out_ref = refs
    for i, ref in enumerate(other_refs):

        @pl.when(pl.program_id(0) == i)
        def _():
            out_ref[0] = ref[...]


def place_others(x, others, held, after=()):
    rows, cols = others[0].shape
    return launch(
        place_kernel,
        [*others, held],
        [(held.shape, held.dtype)],
        grid=(len(others),),
        in_specs=[pl.BlockSpec((rows, cols), lambda r, x: (0, 0))] * len(others)
        + [pl.BlockSpec(memory_space=pl.ANY)],
        out_specs=[pl.BlockSpec((1, rows, cols), lambda r, x: (1 - x[0], 0, r))],
        scalars=(x.reshape(1),),
        aliases={1 + len(others): 0},
        after=after,
    )[0]


def merge_kernel(x_ref, own_ref, other_ref, later_ref, out_ref):
    rows, features = out_ref.shape
    count = own_ref.shape[0]
    t = lax.broadcasted_iota(jnp.int32, (rows, count), 0) + SHORT - 1
    u = lax.broadcasted_iota(jnp.int32, (rows, count), 1)
    e = lax.broadcasted_iota(jnp.int32, (rows, later_ref.shape[0]), 0) + SHORT - 1
    v = lax.broadcasted_iota(jnp.int32, (rows, later_ref.shape[0]), 1)
    x = x_ref[0]
    picks = [
        jnp.where(t == SHORT * u + 2 * side + q, 1.0, 0.0).astype(bf16)
        for side in (x, 1 - x)
        for q in range(2)
    ]
    tail = jnp.where(e == rows + v, 1.0, 0.0).astype(bf16)
    step = 512
    for at in range(0, features, step):
        total = jnp.dot(tail, later_ref[:, at : at + step], preferred_element_type=f32)
        for i, ref in enumerate((own_ref, own_ref, other_ref, other_ref)):
            plane = ref[:, i % 2 * features + at : i % 2 * features + at + step]
            total += jnp.dot(picks[i], plane, preferred_element_type=f32)
        out_ref[:, at : at + step] = total.astype(bf16)


def merge(x, own, other, later, after=()):
    rows = own.shape[0] * SHORT
    return launch(
        merge_kernel,
        [own, other, later],
        [((rows, own.shape[1] // 2), bf16)],
        scalars=(x.reshape(1),),
        after=after,
        limit=20,
    )[0]


SPANS = (3, 9, 4, 4)


def per_device(shortening_input, coarse_grad, weight_copy, master, moment, second):
    fine = shortening_input[0]
    grad = coarse_grad[0]
    weights = weight_copy[0]
    state = (master[0], moment[0], second[0])
    rows_dev, features = fine.shape
    coarse_rows, width = grad.shape
    half_rows = weights.shape[0]
    one = rows_dev // SHORT
    block = master.shape[1]
    n_seq, n_mp = lax.axis_size("seq"), lax.axis_size("mp")
    far = n_seq // 2
    x, z, m = lax.axis_index("dp"), lax.axis_index("seq"), lax.axis_index("mp")
    h, l = z // 2, z % 2
    cols = width // PIECES
    order = (3, 1, 2, 0)

    def place(dp, hi, lo):
        offset = dp * half_rows + (2 * hi + lo) * block
        return [offset // features, offset % features // block]

    def cut(hi, sizes, after):
        places = [place(x, hi, l), place(x, hi, 1 - l), place(1 - x, hi, l), place(1 - x, hi, 1 - l)]
        places = jnp.stack([v for p in places for v in p]).astype(jnp.int32)
        return launch(
            functools.partial(split_kernel, one, block),
            [fine],
            [((size * one, block), bf16) for size in sizes],
            scalars=(places,),
            after=after,
        )

    def diagonal(v):
        return lax.ppermute(v, ("dp", "seq"), [(i, i ^ n_seq ^ 1) for i in range(2 * n_seq)])

    def ahead(v, k):
        return lax.ppermute(v, "seq", [(s, (s + 2 * k) % n_seq) for s in range(n_seq)])

    pair_weights = swap(weights, "mp", 1)
    pair_send, own_rows, g0, g_later = launch(
        functools.partial(sort_kernel, order),
        [grad],
        [((2 * one, width), bf16)] * 2
        + [((coarse_rows, cols), bf16), ((coarse_rows, width - cols), bf16)],
        scalars=(m.reshape(1),),
    )
    g0_dp = swap(g0, "dp", 1)
    first = {}
    last = g0
    for k in range(1, far):
        own, to_seq, to_dp, to_both = cut((h + k) % far, (1, 1, 1, 1), [last])
        first[k] = own, swap(to_dp, "dp", 1), swap(to_seq, "seq", 1), diagonal(to_both)
        last = own
    for k, (own, dp, seq, both) in first.items():
        (three,) = stack([[(i, 0, one) for i in range(3)]], own, dp, seq, after=[last])
        first[k] = three, both, swap(three, "mp", 2), swap(both, "mp", 2), swap(three, "mp", 1)
        last = three
    (pack,) = stack(
        [[(0, 0, coarse_rows), (1, 0, coarse_rows)]], g0, g0_dp, after=[last, pair_weights] + [v[1] for v in first.values()]
    )
    packs = [swap(pack, "seq", 1)]
    first = {k: (*v, swap(v[1], "mp", 1)) for k, v in first.items()}
    last = pack
    later_dp = swap(g_later, "dp", 1)
    own_pair = swap(pair_send, "mp", 1)
    other_send, other_rows, *later_packs = launch(
        halves_kernel,
        [g_later, g0_dp, later_dp],
        [((2 * one, width), bf16)] * 2 + [((2 * coarse_rows, cols), bf16)] * (PIECES - 1),
        after=[last, packs[0]] + [w for v in first.values() for w in v[4:]],
    )
    packs += [swap(v, "seq", 1) for v in later_packs]
    other_pair = swap(other_send, "mp", 1)
    own, to_seq, to_dp = cut(h, (1, 1, 2), [other_rows])
    x_dp = swap(to_dp, "dp", 1)
    last = own
    x_far = {}
    for k, (three, both, *came) in first.items():
        across, across_both, beside, beside_both = came
        x_far[k] = (
            [swap(across, "mp", 1), swap(across_both, "mp", 1)],
            [beside, beside_both],
            [across, across_both],
            [three, both],
        )

    def gradients(i):
        if i == 0:
            return [g0, g0_dp, packs[0]], [(0, 0, 0), (1, 0, 0), (2, 0, 0), (2, coarse_rows, 0)]
        at = (i - 1) * cols
        return [g_later, later_dp, packs[i]], [(0, 0, at), (1, 0, at), (2, 0, 0), (2, coarse_rows, 0)]

    def far_sums(i, after):
        came = []
        for k, v in x_far.items():
            sent = against(v, gradients(i), cols, bf16, after=after)
            came.append(ahead(sent, k))
            after = [sent]
        return (came[0] if far == 2 else sum(v.astype(f32) for v in came)), sent

    sums = {}
    sums[0], last = far_sums(0, [last])
    *other_send, other_rest = act_products([other_rows, other_pair], [weights, pair_weights], [last])
    other_came = [swap(v, "mp", 2) for v in other_send]
    last = other_rest

    sums[1], last = far_sums(1, [last])
    near, to_seq = stack(
        [[(0, 0, one), (2, 0, one)], [(1, 0, one), (2, one, one)]], own, to_seq, x_dp, after=[last]
    )
    x_seq = swap(to_seq, "seq", 1)
    last = mark(SPANS[0], near, sums[0])
    (mine,) = stack([[(0, 0, 2 * one), (1, 0, 2 * one)]], near, x_seq, after=[last])
    across, beside = swap(mine, "mp", 2), swap(mine, "mp", 1)
    act_other = last_sum(other_rest, other_came, after=[mine])
    act_other_came = swap(act_other, "dp", 1)
    *own_send, own_rest = act_products([own_rows, own_pair], [weights, pair_weights], [act_other])
    own_came = [swap(v, "mp", 2) for v in own_send]
    last = mark(SPANS[1], own_rest, sums[1], packs[2])
    (across,) = stack([[(0, 0, 4 * one)]], across, after=[last, act_other_came, beside])
    sums[2], last = far_sums(2, [across])
    both = swap(across, "mp", 1)
    x_near = [both], [beside], [across], [mine]
    scale = 1.0 / math.sqrt(lax.axis_size("dp") * coarse_rows * n_seq)
    held, others = None, []

    def nearby(i, after):
        return against(x_near, gradients(i), cols, f32, after=after)

    def update(i, gradient, after):
        nonlocal held
        *held, low = adam(x, gradient, sums[i], state, i, scale, held, after=after)
        others.append(swap(low, "dp", 1))
        return low

    last = update(0, nearby(0, [last]), [])
    last = update(1, nearby(1, [last]), [])
    gradient = nearby(2, [last])
    sums[3], last = far_sums(3, [gradient])
    fourth = nearby(3, [last])
    last = mark(SPANS[2], fourth, sums[2])
    last = mark(0, last, *others)
    last = update(2, gradient, [last])

    act_own = last_sum(own_rest, own_came, after=[last])
    head = jnp.where(
        x == 0,
        jnp.concatenate([act_own[:1], act_other_came[:1]], axis=1),
        jnp.concatenate([act_other_came[:1], act_own[:1]], axis=1),
    )
    head = head[:, : (SHORT - 1) * features].reshape(SHORT - 1, features)
    count = n_seq * n_mp
    later = lax.ppermute(head, ("seq", "mp"), [(s, s - 1) for s in range(1, count)])
    later = jnp.pad(later, ((0, 16 - (SHORT - 1)), (0, 0)))
    act_grad = merge(x, act_own, act_other_came, later)
    last = mark(SPANS[3], act_grad, sums[3])
    last = mark(0, last, others[2])
    update(3, fourth, [last])
    held[3] = place_others(x, others, held[3])
    new_master, new_moment, new_second, new_weight = held
    return (act_grad[None], new_master[None], new_moment[None], new_second[None], new_weight)


def solution(mesh):
    return jax.shard_map(
        per_device,
        mesh=mesh,
        in_specs=(
            P("dp", ("seq", "mp"), None),
            P("dp", "seq", "mp"),
            P("dp", None, "mp"),
            P("dp", "seq", "mp"),
            P("dp", "seq", "mp"),
            P("dp", "seq", "mp"),
        ),
        out_specs=(
            P("dp", ("seq", "mp"), None),
            P("dp", "seq", "mp"),
            P("dp", "seq", "mp"),
            P("dp", "seq", "mp"),
            P(None, "seq", "mp"),
        ),
        check_vma=False,
    )
```

```python
import functools
import math

import jax
import jax.numpy as jnp
from jax import lax
from jax.experimental import pallas as pl
from jax.experimental.pallas import tpu as pltpu
from jax.sharding import PartitionSpec as P

SHORT = 4
first_beta = 0.9
second_beta = 0.95
first_fix = 1.0 - 0.9**10
second_fix = 1.0 - 0.95**10
adam_eps = 1e-08
learn_rate = 0.05
weight_decay = 0.1
PIECES = 4

bf16, f32 = jnp.bfloat16, jnp.float32


def swap(value, axis, step):
    count = lax.axis_size(axis)
    return lax.ppermute(value, axis, [(i, i ^ step) for i in range(count)])


def launch(kernel, values, out, grid=(), in_specs=None, out_specs=None, scalars=(), aliases=None, after=(), limit=14, span=0):
    whole = pl.BlockSpec(memory_space=pltpu.VMEM)
    taken = len(scalars) + len(values)

    def body(*refs):
        kernel(*refs[:taken], *refs[taken + len(after) :])

    return pl.pallas_call(
        body,
        grid_spec=pltpu.PrefetchScalarGridSpec(
            num_scalar_prefetch=len(scalars),
            grid=grid,
            in_specs=(in_specs or [whole] * len(values))
            + [pl.BlockSpec(memory_space=pl.ANY)] * len(after),
            out_specs=out_specs or [whole] * len(out),
        ),
        out_shape=[jax.ShapeDtypeStruct(shape, dtype) for shape, dtype in out],
        input_output_aliases=aliases or {},
        compiler_params=pltpu.CompilerParams(vmem_limit_bytes=limit * 2**20),
        cost_estimate=pl.CostEstimate(flops=1 + span * 1200000000, bytes_accessed=1 + span * 3500000, transcendentals=0),
    )(*scalars, *values, *after)


def mark_kernel(out_ref):
    out_ref[...] = jnp.zeros_like(out_ref)


def mark(span, *after):
    return launch(mark_kernel, [], [((8, 128), f32)], after=after, span=span)[0]


def sort_kernel(order, m_ref, grad_ref, sent_ref, kept_ref, *piece_refs):
    count = grad_ref.shape[0] // len(order)
    half = len(order) // 2
    for i, j in enumerate(order):
        start = pl.multiple_of((m_ref[0] ^ j) * count, count)
        rows = grad_ref[pl.ds(start, count), :]
        ref, at = (sent_ref, i) if i < half else (kept_ref, i - half)
        ref[at * count : (at + 1) * count, :] = rows
        first = 0
        for ref in piece_refs:
            ref[i * count : (i + 1) * count, :] = rows[:, first : first + ref.shape[1]]
            first += ref.shape[1]


def halves_kernel(own_ref, first_ref, later_ref, sent_ref, kept_ref, *pack_refs):
    count, split = sent_ref.shape[0], first_ref.shape[1]
    for ref, part in ((sent_ref, slice(0, count)), (kept_ref, slice(count, 2 * count))):
        ref[:, :split] = first_ref[part]
        ref[:, split:] = later_ref[part]
    for i, ref in enumerate(pack_refs):
        at = slice(i * ref.shape[1], (i + 1) * ref.shape[1])
        ref[: 2 * count] = own_ref[:, at]
        ref[2 * count :] = later_ref[:, at]


def split_kernel(rows, block, at_ref, fine_ref, *out_refs):
    count = fine_ref.shape[0]
    r = lax.broadcasted_iota(jnp.int32, (rows, count), 0)
    t = lax.broadcasted_iota(jnp.int32, (rows, count), 1)
    i = 0
    for out_ref in out_refs:
        for k in range(out_ref.shape[0] // rows):
            pick = jnp.where(t == SHORT * r + at_ref[2 * i], 1.0, 0.0).astype(bf16)
            columns = pl.ds(pl.multiple_of(at_ref[2 * i + 1] * block, block), block)
            out_ref[k * rows : (k + 1) * rows, :] = jnp.dot(
                pick, fine_ref[:, columns], preferred_element_type=f32
            ).astype(bf16)
            i += 1


def stack_kernel(picks, *refs):
    count = len(refs) - len(picks)
    for pick, out_ref in zip(picks, refs[count:]):
        at = 0
        for i, first, size in pick:
            out_ref[at : at + size, :] = refs[i][first : first + size, :]
            at += size


def stack(picks, *values, after=()):
    out = [
        ((sum(size for _, _, size in pick), values[pick[0][0]].shape[1]), bf16) for pick in picks
    ]
    return launch(functools.partial(stack_kernel, picks), values, out, after=after)


def act_kernel(a_ref, b_ref, w_ref, pair_ref, *out_refs):
    *send_refs, rest_ref = out_refs
    count = rest_ref.shape[0]
    product = 0.0
    for rows, part in ((a_ref, w_ref), (b_ref, pair_ref)):
        product += lax.dot_general(
            rows[...], part[...], (((1,), (1,)), ((), ())), preferred_element_type=f32
        )
    rest_ref[...] = product[count:]
    half = pl.num_programs(0) // 2
    for i, ref in enumerate(send_refs):

        @pl.when(pl.program_id(0) // half == i)
        def _():
            ref[...] = product[:count].astype(bf16)


def act_products(rows, weights, after=()):
    count = rows[0].shape[0] // 2
    wide, depth = weights[0].shape
    step = 512
    half = wide // step // 2
    return launch(
        act_kernel,
        [*rows, *weights],
        [((count, wide // 2), bf16)] * 2 + [((count, wide), f32)],
        grid=(wide // step,),
        in_specs=[pl.BlockSpec(v.shape, lambda i: (0, 0)) for v in rows]
        + [pl.BlockSpec((step, depth), lambda i: (i, 0))] * 2,
        out_specs=[
            pl.BlockSpec((count, step), lambda i: (0, jnp.minimum(i, half - 1))),
            pl.BlockSpec((count, step), lambda i: (0, jnp.maximum(i - half, 0))),
            pl.BlockSpec((count, step), lambda i: (0, i)),
        ],
        after=after,
        limit=46,
    )


def last_kernel(keep_ref, *refs):
    *came_refs, out_ref = refs
    at = 0
    for ref in came_refs:
        part = slice(at, at + ref.shape[1])
        out_ref[:, part] = (keep_ref[:, part] + ref[...].astype(f32)).astype(bf16)
        at += ref.shape[1]


def last_sum(keep, came, after=()):
    return launch(last_kernel, [keep, *came], [(keep.shape, bf16)], after=after)[0]


def against_kernel(groups, places, *refs):
    x_refs, g_refs, out_ref = refs[: sum(groups)], refs[sum(groups) : -1], refs[-1]
    count = sum(ref.shape[0] for ref in x_refs[: groups[0]]) // len(places)
    total, first = None, 0
    for j, size in enumerate(groups):
        x = jnp.concatenate([ref[...] for ref in x_refs[first : first + size]], axis=0)
        first += size
        g = jnp.concatenate(
            [
                g_refs[i][row + j * count : row + (j + 1) * count, at : at + out_ref.shape[1]]
                for i, row, at in places
            ],
            axis=0,
        )
        part = lax.dot_general(x, g, (((0,), (0,)), ((), ())), preferred_element_type=f32)
        total = part if total is None else total + part
    out_ref[...] = total.astype(out_ref.dtype)


def against(x, g, cols, dtype, after=()):
    values, places = g
    groups = [len(v) for v in x]
    flat = [v for group in x for v in group]
    return launch(
        functools.partial(against_kernel, groups, places),
        [*flat, *values],
        [((flat[0].shape[1], cols), dtype)],
        after=after,
        limit=20,
    )[0]


def adam_kernel(scale, first, *refs):
    x_ref, own, came, master, moment, second = refs[:6]
    new_master, new_moment, new_second, new_weight, low = refs[6 if first else 10 :]
    gradient = (own[...] + came[...].astype(f32)) * scale
    m = first_beta * moment[...] + (1.0 - first_beta) * gradient
    s = second_beta * second[...] + (1.0 - second_beta) * gradient * gradient
    ratio = m / first_fix / (jnp.sqrt(s / second_fix) + adam_eps)
    w = master[...] - learn_rate * (ratio + weight_decay * master[...])
    new_master[...] = w
    new_moment[...] = m
    new_second[...] = s
    low[...] = w.astype(bf16)
    new_weight[0] = w.astype(bf16)


def adam(x, own, came, state, i, scale, held, after=()):
    rows, cols = own.shape
    wide = state[0].shape[1]
    step = min(256, rows)
    local = pl.BlockSpec((step, cols), lambda r, x: (r, 0))
    whole = pl.BlockSpec((step, cols), lambda r, x: (r, i))
    weight = pl.BlockSpec((1, step, cols), lambda r, x: (x[0], r, i))
    first = held is None
    return launch(
        functools.partial(adam_kernel, scale, first),
        [own, came, *state, *(held or ())],
        [((rows, wide), f32)] * 3 + [((2, rows, wide), bf16), ((rows, cols), bf16)],
        grid=(rows // step,),
        in_specs=[local, local, whole, whole, whole]
        + ([] if first else [pl.BlockSpec(memory_space=pl.ANY)] * 4),
        out_specs=[whole, whole, whole, weight, local],
        scalars=(x.reshape(1),),
        aliases={} if first else {6: 0, 7: 1, 8: 2, 9: 3},
        after=after,
    )


def place_kernel(x_ref, *refs):
    *other_refs, held_ref, out_ref = refs
    for i, ref in enumerate(other_refs):

        @pl.when(pl.program_id(0) == i)
        def _():
            out_ref[0] = ref[...]


def place_others(x, others, held, after=()):
    rows, cols = others[0].shape
    return launch(
        place_kernel,
        [*others, held],
        [(held.shape, held.dtype)],
        grid=(len(others),),
        in_specs=[pl.BlockSpec((rows, cols), lambda r, x: (0, 0))] * len(others)
        + [pl.BlockSpec(memory_space=pl.ANY)],
        out_specs=[pl.BlockSpec((1, rows, cols), lambda r, x: (1 - x[0], 0, r))],
        scalars=(x.reshape(1),),
        aliases={1 + len(others): 0},
        after=after,
    )[0]


def merge_kernel(x_ref, own_ref, other_ref, later_ref, out_ref):
    rows, features = out_ref.shape
    count = own_ref.shape[0]
    t = lax.broadcasted_iota(jnp.int32, (rows, count), 0) + SHORT - 1
    u = lax.broadcasted_iota(jnp.int32, (rows, count), 1)
    e = lax.broadcasted_iota(jnp.int32, (rows, later_ref.shape[0]), 0) + SHORT - 1
    v = lax.broadcasted_iota(jnp.int32, (rows, later_ref.shape[0]), 1)
    x = x_ref[0]
    picks = [
        jnp.where(t == SHORT * u + 2 * side + q, 1.0, 0.0).astype(bf16)
        for side in (x, 1 - x)
        for q in range(2)
    ]
    tail = jnp.where(e == rows + v, 1.0, 0.0).astype(bf16)
    step = 512
    for at in range(0, features, step):
        total = jnp.dot(tail, later_ref[:, at : at + step], preferred_element_type=f32)
        for i, ref in enumerate((own_ref, own_ref, other_ref, other_ref)):
            plane = ref[:, i % 2 * features + at : i % 2 * features + at + step]
            total += jnp.dot(picks[i], plane, preferred_element_type=f32)
        out_ref[:, at : at + step] = total.astype(bf16)


def merge(x, own, other, later, after=()):
    rows = own.shape[0] * SHORT
    return launch(
        merge_kernel,
        [own, other, later],
        [((rows, own.shape[1] // 2), bf16)],
        scalars=(x.reshape(1),),
        after=after,
        limit=20,
    )[0]


SPANS = (3, 9, 4, 4)


def per_device(shortening_input, coarse_grad, weight_copy, master, moment, second):
    fine = shortening_input[0]
    grad = coarse_grad[0]
    weights = weight_copy[0]
    state = (master[0], moment[0], second[0])
    rows_dev, features = fine.shape
    coarse_rows, width = grad.shape
    half_rows = weights.shape[0]
    one = rows_dev // SHORT
    block = master.shape[1]
    n_seq, n_mp = lax.axis_size("seq"), lax.axis_size("mp")
    far = n_seq // 2
    x, z, m = lax.axis_index("dp"), lax.axis_index("seq"), lax.axis_index("mp")
    h, l = z // 2, z % 2
    cols = width // PIECES
    order = (3, 1, 2, 0)

    def place(dp, hi, lo):
        offset = dp * half_rows + (2 * hi + lo) * block
        return [offset // features, offset % features // block]

    def cut(hi, sizes, after):
        places = [place(x, hi, l), place(x, hi, 1 - l), place(1 - x, hi, l), place(1 - x, hi, 1 - l)]
        places = jnp.stack([v for p in places for v in p]).astype(jnp.int32)
        return launch(
            functools.partial(split_kernel, one, block),
            [fine],
            [((size * one, block), bf16) for size in sizes],
            scalars=(places,),
            after=after,
        )

    def diagonal(v):
        return lax.ppermute(v, ("dp", "seq"), [(i, i ^ n_seq ^ 1) for i in range(2 * n_seq)])

    def ahead(v, k):
        return lax.ppermute(v, "seq", [(s, (s + 2 * k) % n_seq) for s in range(n_seq)])

    pair_weights = swap(weights, "mp", 1)
    pair_send, own_rows, g0, g_later = launch(
        functools.partial(sort_kernel, order),
        [grad],
        [((2 * one, width), bf16)] * 2
        + [((coarse_rows, cols), bf16), ((coarse_rows, width - cols), bf16)],
        scalars=(m.reshape(1),),
    )
    g0_dp = swap(g0, "dp", 1)
    first = {}
    last = g0
    for k in range(1, far):
        own, to_seq, to_dp, to_both = cut((h + k) % far, (1, 1, 1, 1), [last])
        first[k] = own, swap(to_dp, "dp", 1), swap(to_seq, "seq", 1), diagonal(to_both)
        last = own
    for k, (own, dp, seq, both) in first.items():
        (three,) = stack([[(i, 0, one) for i in range(3)]], own, dp, seq, after=[last])
        first[k] = three, both, swap(three, "mp", 2), swap(both, "mp", 2), swap(three, "mp", 1)
        last = three
    (pack,) = stack(
        [[(0, 0, coarse_rows), (1, 0, coarse_rows)]], g0, g0_dp, after=[last, pair_weights] + [v[1] for v in first.values()]
    )
    packs = [swap(pack, "seq", 1)]
    first = {k: (*v, swap(v[1], "mp", 1)) for k, v in first.items()}
    last = pack
    later_dp = swap(g_later, "dp", 1)
    own_pair = swap(pair_send, "mp", 1)
    other_send, other_rows, *later_packs = launch(
        halves_kernel,
        [g_later, g0_dp, later_dp],
        [((2 * one, width), bf16)] * 2 + [((2 * coarse_rows, cols), bf16)] * (PIECES - 1),
        after=[last, packs[0]] + [w for v in first.values() for w in v[4:]],
    )
    packs += [swap(v, "seq", 1) for v in later_packs]
    other_pair = swap(other_send, "mp", 1)
    own, to_seq, to_dp = cut(h, (1, 1, 2), [other_rows])
    x_dp = swap(to_dp, "dp", 1)
    last = own
    x_far = {}
    for k, (three, both, *came) in first.items():
        across, across_both, beside, beside_both = came
        x_far[k] = (
            [swap(across, "mp", 1), swap(across_both, "mp", 1)],
            [beside, beside_both],
            [across, across_both],
            [three, both],
        )

    def gradients(i):
        if i == 0:
            return [g0, g0_dp, packs[0]], [(0, 0, 0), (1, 0, 0), (2, 0, 0), (2, coarse_rows, 0)]
        at = (i - 1) * cols
        return [g_later, later_dp, packs[i]], [(0, 0, at), (1, 0, at), (2, 0, 0), (2, coarse_rows, 0)]

    def far_sums(i, after):
        came = []
        for k, v in x_far.items():
            sent = against(v, gradients(i), cols, bf16, after=after)
            came.append(ahead(sent, k))
            after = [sent]
        return (came[0] if far == 2 else sum(v.astype(f32) for v in came)), sent

    sums = {}
    sums[0], last = far_sums(0, [last])
    near, to_seq = stack(
        [[(0, 0, one), (2, 0, one)], [(1, 0, one), (2, one, one)]], own, to_seq, x_dp, after=[last]
    )
    *other_send, other_rest = act_products([other_rows, other_pair], [weights, pair_weights], [near])
    other_came = [swap(v, "mp", 2) for v in other_send]
    last = other_rest

    sums[1], last = far_sums(1, [last])
    x_seq = swap(to_seq, "seq", 1)
    last = mark(SPANS[0], last, sums[0])
    (mine,) = stack([[(0, 0, 2 * one), (1, 0, 2 * one)]], near, x_seq, after=[last])
    across, beside = swap(mine, "mp", 2), swap(mine, "mp", 1)
    act_other = last_sum(other_rest, other_came, after=[mine])
    act_other_came = swap(act_other, "dp", 1)
    *own_send, own_rest = act_products([own_rows, own_pair], [weights, pair_weights], [act_other])
    own_came = [swap(v, "mp", 2) for v in own_send]
    last = mark(SPANS[1], own_rest, sums[1], packs[2])
    (across,) = stack([[(0, 0, 4 * one)]], across, after=[last, act_other_came, beside])
    sums[2], last = far_sums(2, [across])
    both = swap(across, "mp", 1)
    x_near = [both], [beside], [across], [mine]
    scale = 1.0 / math.sqrt(lax.axis_size("dp") * coarse_rows * n_seq)
    held, others = None, []

    def nearby(i, after):
        return against(x_near, gradients(i), cols, f32, after=after)

    def update(i, gradient, after):
        nonlocal held
        *held, low = adam(x, gradient, sums[i], state, i, scale, held, after=after)
        others.append(swap(low, "dp", 1))
        return low

    last = update(0, nearby(0, [last]), [])
    last = update(1, nearby(1, [last]), [])
    gradient = nearby(2, [last])
    sums[3], last = far_sums(3, [gradient])
    fourth = nearby(3, [last])
    last = mark(SPANS[2], fourth, sums[2])
    last = mark(0, last, *others)
    last = update(2, gradient, [last])

    act_own = last_sum(own_rest, own_came, after=[last])
    head = jnp.where(
        x == 0,
        jnp.concatenate([act_own[:1], act_other_came[:1]], axis=1),
        jnp.concatenate([act_other_came[:1], act_own[:1]], axis=1),
    )
    head = head[:, : (SHORT - 1) * features].reshape(SHORT - 1, features)
    count = n_seq * n_mp
    later = lax.ppermute(head, ("seq", "mp"), [(s, s - 1) for s in range(1, count)])
    later = jnp.pad(later, ((0, 16 - (SHORT - 1)), (0, 0)))
    act_grad = merge(x, act_own, act_other_came, later)
    last = mark(SPANS[3], act_grad, sums[3])
    last = mark(0, last, others[2])
    update(3, fourth, [last])
    held[3] = place_others(x, others, held[3])
    new_master, new_moment, new_second, new_weight = held
    return (act_grad[None], new_master[None], new_moment[None], new_second[None], new_weight)


def solution(mesh):
    return jax.shard_map(
        per_device,
        mesh=mesh,
        in_specs=(
            P("dp", ("seq", "mp"), None),
            P("dp", "seq", "mp"),
            P("dp", None, "mp"),
            P("dp", "seq", "mp"),
            P("dp", "seq", "mp"),
            P("dp", "seq", "mp"),
        ),
        out_specs=(
            P("dp", ("seq", "mp"), None),
            P("dp", "seq", "mp"),
            P("dp", "seq", "mp"),
            P("dp", "seq", "mp"),
            P(None, "seq", "mp"),
        ),
        check_vma=False,
    )
```
